128 devices in a mesh: resp: 16 (over z, x_hi, core), ctx: 8 (over y, x_lo).
Axes of the slice: x: 4 (x_hi: 2, x_lo: 2; x = x_hi * 2 + x_lo), y: 4, z: 4, core: 2. Of those that a mesh axis runs over, the one named last changes fastest.
Arguments:
- queries: bfloat16 [16, 1024, 8192], P('resp', 'ctx'), may hold values from -5 to 5
- resp_keys: bfloat16 [16, 1024, 1024], P('resp', 'ctx'), may hold values from -5 to 5
- resp_values: bfloat16 [16, 1024, 1024], P('resp', 'ctx'), may hold values from -6 to 6
- prompt_keys: bfloat16 [256, 1024], P(('resp', 'ctx')), may hold values from -5 to 5
- prompt_values: bfloat16 [256, 1024], P(('resp', 'ctx')), may hold values from -6 to 6
- upstream: bfloat16 [16, 1024, 8192], P('resp', 'ctx'), may hold values from -6 to 6
- lengths: int32 [16], P('resp'), may hold values from 256 to 1024, as said below
- prompt_length: int32 [1], replicated, may hold values from 64 to 256
Outputs:
- attended: bfloat16 [16, 1024, 8192], P('resp', 'ctx')
- query_grads: bfloat16 [16, 1024, 8192], P('resp', 'ctx')
- key_grads: float32 [16, 1024, 1024], P('resp', 'ctx')
- value_grads: float32 [16, 1024, 1024], P('resp', 'ctx')
- prompt_keygrad: float32 [256, 1024], P(('resp', 'ctx'))
- prompt_valuegrad: float32 [256, 1024], P(('resp', 'ctx'))
The draws below stay inside these ranges and needn't reach their ends.
Inputs may be any that keep to these rules, and one draw needn't show every extreme that they name: `lengths`: one response is live over all 1024 positions and one over exactly 256.
All inputs are finite; a program needn't handle non-finite values.
Results may differ from the reference program's by a relative error of at most 0.025.
Values may be sent and summed in bfloat16 or wider, within the bound.
A program may use at most 128 MiB of HBM per device.

```python
import jax
import jax.numpy as jnp
from jax import lax

H = 64
KVH = 8
HD = 128
G = 8
TOK_DEV = 128
RESPONSES = 16
L = 1024
P_SIZE = 256


def draw_queries(key, part):
    key = jax.random.fold_in(key, 11)
    key_base = jax.random.fold_in(key, 0)
    array_shape = (RESPONSES, L, H * HD)
    drawn = jnp.clip(1.4 * jax.random.normal(key_base, array_shape, jnp.float32), -5.0, 5.0)
    return drawn.astype(jnp.bfloat16)


def draw_prompt_keys(key, part):
    key = jax.random.fold_in(key, 12)
    key_base = jax.random.fold_in(key, 0)
    array_shape = (P_SIZE, KVH * HD)
    drawn = jnp.clip(1.4 * jax.random.normal(key_base, array_shape, jnp.float32), -5.0, 5.0)
    return drawn.astype(jnp.bfloat16)


def draw_lengths(key, part):
    key = jax.random.fold_in(key, 13)
    key_draw, key_long, key_short = jax.random.split(key, 3)
    drawn = jax.random.randint(key_draw, (RESPONSES,), L // 4, L + 1)
    longest = jax.random.randint(key_long, (), 0, RESPONSES)
    shortest = (longest + 1 + jax.random.randint(key_short, (), 0, RESPONSES - 1)) % RESPONSES
    response_ids = jnp.arange(RESPONSES)
    drawn = jnp.where(response_ids == longest, L, jnp.where(response_ids == shortest, L // 4, drawn))
    return drawn.astype(jnp.int32)


def block_levels(key, extent, cuts, smallest, top_value):
    loudness = 1.0
    for axis_at, shards_of in cuts:
        steps = jax.random.uniform(jax.random.fold_in(jax.random.fold_in(key, 6), axis_at), (shards_of,), jnp.float32, smallest / len(cuts), top_value / len(cuts))
        loudness = loudness * jnp.repeat(jnp.exp(steps), extent[axis_at] // shards_of).reshape((-1,) + (1,) * (len(extent) - 1 - axis_at))
    return loudness


def centred(rng, shape, spread, limit, cuts=(), kind=jnp.bfloat16):
    factor_of = block_levels(rng, shape, cuts, -0.22, 0.18) if cuts else 1.0
    array = jax.random.normal(rng, shape, jnp.float32) * spread * factor_of
    return jnp.minimum(jnp.maximum(array, -limit), limit).astype(kind)


def setup_inputs(seed: int = 0) -> dict:
    splits = jax.random.split(jax.random.key(seed), 9)
    queries = draw_queries(jax.random.fold_in(splits[8], 71), 0)
    resp_keys = centred(splits[1], (RESPONSES, L, KVH * HD), 1.4, 5.0, ((0, 16), (1, 8)))
    resp_values = centred(splits[2], (RESPONSES, L, KVH * HD), 1.0, 6.0, ((0, 16), (1, 8)))
    prompt_keys = draw_prompt_keys(jax.random.fold_in(splits[8], 71), 0)
    prompt_values = centred(splits[4], (P_SIZE, KVH * HD), 1.0, 6.0, ((0, 128),))
    upstream = centred(splits[5], (RESPONSES, L, H * HD), 1.0, 6.0, ((0, 16), (1, 8)))
    lengths = draw_lengths(jax.random.fold_in(splits[8], 71), 0)
    prompt_length = jax.random.randint(splits[7], (1,), P_SIZE // 4, P_SIZE + 1).astype(jnp.int32)
    return {"queries": queries, "resp_keys": resp_keys, "resp_values": resp_values, "prompt_keys": prompt_keys, "prompt_values": prompt_values, "upstream": upstream, "lengths": lengths, "prompt_length": prompt_length}


def softmax_rows(scores):
    top = jnp.max(scores, axis=-1, keepdims=True)
    expo = jnp.exp(scores - top)
    return expo / jnp.sum(expo, axis=-1, keepdims=True)


def reference(queries, resp_keys, resp_values, prompt_keys, prompt_values, upstream, lengths, prompt_length):
    scaling = HD ** -0.5
    position = jnp.arange(L, dtype=jnp.int32)
    key_index = jnp.arange(P_SIZE + L, dtype=jnp.int32)
    visible = ((key_index < P_SIZE) & (key_index < prompt_length[0]))[None, :] | (
        (key_index >= P_SIZE)[None, :] & (key_index[None, :] - P_SIZE <= position[:, None]))
    blocks = L // TOK_DEV

    def per_response(items):
        query_rows, key_rows, value_rows, grad_rows, length = items
        live = position < length
        masked = jnp.where(live[:, None], grad_rows, jnp.zeros((), grad_rows.dtype))
        keys_all = jnp.concatenate([prompt_keys, key_rows], 0).reshape(P_SIZE + L, KVH, HD).transpose(1, 0, 2)
        values_all = jnp.concatenate([prompt_values, value_rows], 0).reshape(P_SIZE + L, KVH, HD).transpose(1, 0, 2)
        query_heads = query_rows.reshape(L, KVH, G, HD).transpose(1, 0, 2, 3)
        grad_heads = masked.reshape(L, KVH, G, HD).transpose(1, 0, 2, 3)

        def per_group(parts):
            qgroup, ggroup, kgroup, vgroup = parts
            q_wide = qgroup.astype(jnp.float32)
            g_wide = ggroup.astype(jnp.float32)
            k_wide = kgroup.astype(jnp.float32)
            v_wide = vgroup.astype(jnp.float32)
            scores = jnp.einsum("tjd,kd->tjk", q_wide, k_wide) * scaling
            scores = jnp.where(visible[:, None, :], scores, -jnp.inf)
            weights = softmax_rows(scores)
            weights_low = weights.astype(jnp.bfloat16)
            mixed = jnp.einsum("tjk,kd->tjd", weights_low.astype(jnp.float32), v_wide)
            result = jnp.where(live[:, None, None], mixed, 0.0).astype(jnp.bfloat16)
            correction = jnp.sum(g_wide * result.astype(jnp.float32), axis=-1)
            prob_grad = jnp.einsum("tjd,kd->tjk", g_wide, v_wide)
            score_grad = (weights * (prob_grad - correction[..., None]) * scaling).astype(jnp.bfloat16)
            score_wide = score_grad.astype(jnp.float32)
            qgrad = jnp.einsum("tjk,kd->tjd", score_wide, k_wide).astype(jnp.bfloat16)
            key_terms = jnp.einsum("ctjk,ctjd->ckd", score_wide.reshape(blocks, TOK_DEV, G, P_SIZE + L),
                                   q_wide.reshape(blocks, TOK_DEV, G, HD))
            value_terms = jnp.einsum("ctjk,ctjd->ckd",
                                     weights_low.astype(jnp.float32).reshape(blocks, TOK_DEV, G, P_SIZE + L),
                                     g_wide.reshape(blocks, TOK_DEV, G, HD))
            resp_kgrad = jnp.sum(lax.optimization_barrier(key_terms[:, P_SIZE:].astype(jnp.bfloat16)).astype(jnp.float32), 0)
            resp_vgrad = jnp.sum(lax.optimization_barrier(value_terms[:, P_SIZE:].astype(jnp.bfloat16)).astype(jnp.float32), 0)
            prompt_kpart = jnp.sum(key_terms[:, :P_SIZE], 0)
            prompt_vpart = jnp.sum(value_terms[:, :P_SIZE], 0)
            return result, qgrad, resp_kgrad, resp_vgrad, prompt_kpart, prompt_vpart

        outputs = lax.map(per_group, (query_heads, grad_heads, keys_all, values_all))
        result = outputs[0].transpose(1, 0, 2, 3).reshape(L, H * HD)
        qgrad = outputs[1].transpose(1, 0, 2, 3).reshape(L, H * HD)
        kgrad = outputs[2].transpose(1, 0, 2).reshape(L, KVH * HD)
        vgrad = outputs[3].transpose(1, 0, 2).reshape(L, KVH * HD)
        pkgrad = outputs[4].transpose(1, 0, 2).reshape(P_SIZE, KVH * HD)
        pvgrad = outputs[5].transpose(1, 0, 2).reshape(P_SIZE, KVH * HD)
        return result, qgrad, kgrad, vgrad, pkgrad, pvgrad

    results = lax.map(per_response, (queries, resp_keys, resp_values, upstream, lengths))
    prompt_keygrad = jnp.sum(results[4], 0)
    prompt_valuegrad = jnp.sum(results[5], 0)
    return (results[0], results[1], results[2], results[3], prompt_keygrad, prompt_valuegrad)
```

```python
import functools

import jax
import jax.numpy as jnp
from jax import lax
from jax.experimental import pallas as pl
from jax.experimental.pallas import tpu as pltpu
from jax.sharding import PartitionSpec as P

HD = 128
KVH = 8
G = 8
ROWS = G * HD
TOK = 128
SCALE = HD**-0.5
LOG2E = 1.4426950408889634
HIDE = -1e30
NT = (((1,), (1,)), ((), ()))
F32 = jnp.float32
BF = jnp.bfloat16
MESH = pl.DeviceIdType.MESH


def iota(shape, axis):
    return lax.broadcasted_iota(jnp.int32, shape, axis)


def dot(a, b):
    return jnp.dot(a, b, preferred_element_type=F32)


def dot_nt(a, b):
    return lax.dot_general(a, b, NT, preferred_element_type=F32)


def kernel(
    nr, nc,
    q_hbm, d_hbm, k_ref, v_ref, pk_ref, pv_ref, len_ref, plen_ref,
    out_hbm, dq_hbm, kg_ref, vg_ref, pkg_ref, pvg_ref,
    qv, dv, ov, dqv, kv, term, rterm, hidden_cols, ones_cols, causal_cols,
    pown, prep, pterm, psum, pback,
    in_sem, out_sem,
    a_send, a_recv, b_send, b_recv, g_send, g_recv,
    t_send, t_recv, p_send, p_recv, z_send, z_recv,
):
    prow = 2 * nc
    prompt = nr * prow
    key_rows = prompt + nc * TOK
    r = lax.axis_index("resp")
    c = lax.axis_index("ctx")

    load_q = pltpu.make_async_copy(q_hbm, qv, in_sem.at[0])
    load_d = pltpu.make_async_copy(d_hbm, dv, in_sem.at[1])
    load_q.start()
    load_d.start()

    barrier = pltpu.get_barrier_semaphore()

    def others(n, me, body):
        def step(i, carry):
            body(lax.rem(me + i, n))
            return carry

        lax.fori_loop(1, n, step, 0)

    others(nc, c, lambda p: pl.semaphore_signal(barrier, inc=1, device_id={"ctx": p}, device_id_type=MESH))
    others(nr, r, lambda p: pl.semaphore_signal(barrier, inc=1, device_id={"resp": p}, device_id_type=MESH))

    def block_rows(j):
        return pl.ds(pl.multiple_of(prompt + j * TOK, TOK), TOK)

    pown[c, 0] = pk_ref[...]
    pown[c, 1] = pv_ref[...]
    for g in range(KVH):
        kv[g, 0, block_rows(c), :] = k_ref[:, g * HD:(g + 1) * HD]
        kv[g, 1, block_rows(c), :] = v_ref[:, g * HD:(g + 1) * HD]

    pl.semaphore_wait(barrier, nc - 1 + nr - 1)

    def copy_a(slot, peer):
        return pltpu.make_async_remote_copy(
            src_ref=pown.at[slot], dst_ref=pown.at[slot],
            send_sem=a_send.at[peer], recv_sem=a_recv.at[slot],
            device_id={"ctx": peer}, device_id_type=MESH)

    others(nc, c, lambda p: copy_a(c, p).start())

    def copy_g(g, slot, peer):
        return pltpu.make_async_remote_copy(
            src_ref=kv.at[g, :, block_rows(slot), :], dst_ref=kv.at[g, :, block_rows(slot), :],
            send_sem=g_send.at[g, peer], recv_sem=g_recv.at[g, slot],
            device_id={"ctx": peer}, device_id_type=MESH)

    def loop(lo, hi, body):
        def step(i, carry):
            body(i)
            return carry

        lax.fori_loop(lo, hi, step, 0)

    loop(0, KVH, lambda g: loop(c + 1, nc, lambda p: copy_g(g, c, p).start()))

    def clear(j):
        def one(g):
            kv[g, 0, block_rows(j), :] = jnp.zeros((TOK, HD), BF)
            kv[g, 1, block_rows(j), :] = jnp.zeros((TOK, HD), BF)
        loop(0, KVH, one)

    loop(c + 1, nc, clear)

    row = iota((key_rows, HD), 0)
    col = iota((key_rows, HD), 1)
    gone = ((row < prompt) & (row >= plen_ref[0])) | (row >= prompt + (c + 1) * TOK)
    diagonal = (row - (prompt + c * TOK) == col) & (col > 0)
    hidden_cols[...] = jnp.where(diagonal, 1.0, jnp.where(gone & (col == 0), HIDE, 0.0)).astype(BF)
    ones_cols[...] = jnp.where(col < 2, 1.0, 0.0).astype(BF)
    tok = iota((TOK, HD), 0)
    key = iota((TOK, HD), 1)
    causal_cols[...] = jnp.where(key == 0, 1.0, jnp.where(key > tok, HIDE, 0.0)).astype(BF)
    live = c * TOK + tok < len_ref[0]
    live_lane = jnp.where(c * TOK + iota((1, TOK), 1) < len_ref[0], 1.0, 0.0)

    n16 = 16 * nc

    def order(to_heads):
        a = iota((n16, n16), 0)
        b = iota((n16, n16), 1)
        if not to_heads:
            a, b = b, a
        head, rest = a // prow, lax.rem(a, prow)
        return jnp.where(rest * KVH + head == b, 1.0, 0.0).astype(BF)

    to_heads = order(True)
    others(nc, c, lambda p: copy_a(p, p).wait_recv())
    my_rows = pl.ds(pl.multiple_of(r * prow, prow), prow)
    for w in range(2):
        got = jnp.concatenate([pown[j, w] for j in range(nc)], 0)
        mine = dot(to_heads, got).astype(BF)
        for g in range(KVH):
            kv[g, w, my_rows, :] = mine[g * prow:(g + 1) * prow]

    pieces = ((0, 1), (1, 2), (3, 5))

    def copy_b(n, slot, peer):
        g0, count = pieces[n]
        rows = pl.ds(pl.multiple_of(slot * prow, prow), prow)
        part = kv.at[pl.ds(g0, count), :, rows, :]
        return pltpu.make_async_remote_copy(
            src_ref=part, dst_ref=part,
            send_sem=b_send.at[n, peer], recv_sem=b_recv.at[n, slot],
            device_id={"resp": peer}, device_id_type=MESH)

    for n in range(len(pieces)):
        others(nr, r, lambda p: copy_b(n, r, p).start())

    load_q.wait()
    load_d.wait()

    def copy_t(g, block, src):
        return pltpu.make_async_remote_copy(
            src_ref=term.at[g, :, block_rows(block), :], dst_ref=rterm.at[src, g],
            send_sem=t_send.at[g, block], recv_sem=t_recv.at[g, src],
            device_id={"ctx": block}, device_id_type=MESH)

    def copy_p(n, owner, src):
        rows = pl.ds(pl.multiple_of(owner * prow, prow), prow)
        return pltpu.make_async_remote_copy(
            src_ref=term.at[pl.ds(2 * n, 2), :, rows, :], dst_ref=pterm.at[src, pl.ds(2 * n, 2)],
            send_sem=p_send.at[n, owner], recv_sem=p_recv.at[n, src],
            device_id={"resp": owner}, device_id_type=MESH)

    def store_out(g, which):
        cols = pl.ds(pl.multiple_of(g * ROWS, ROWS), ROWS)
        src, dst = ((ov, out_hbm), (dqv, dq_hbm))[which]
        return pltpu.make_async_copy(src.at[:, cols], dst.at[:, cols], out_sem.at[which, g])

    def head(g):
        for n, (g0, _) in enumerate(pieces):
            @pl.when(g == g0)
            def _():
                others(nr, r, lambda p: copy_b(n, p, p).wait_recv())
        loop(0, c, lambda j: copy_g(g, j, j).wait_recv())

        cols = [pl.ds(pl.multiple_of(g * ROWS + a * HD, HD), HD) for a in range(G)]
        k = kv[g, 0]
        v = kv[g, 1]
        q = jnp.concatenate([qv[:, x] for x in cols], 0)
        d = jnp.concatenate([jnp.where(live, dv[:, x], jnp.zeros((), BF)) for x in cols], 0)
        limit = jnp.concatenate([causal_cols[...]] * G, 0)
        s = dot_nt(jnp.concatenate([k, hidden_cols[...]], 1), jnp.concatenate([q, limit], 1))
        top = jnp.max(s, 0, keepdims=True)
        p = jnp.exp2((s - top) * (SCALE * LOG2E))
        inv = 1.0 / jnp.sum(p, 0, keepdims=True)
        p = p.astype(BF)
        out = dot(v.T, p) * (inv * jnp.concatenate([live_lane] * G, 1))
        out = out.T.astype(BF)
        for a in range(G):
            ov[:, cols[a]] = out[a * TOK:(a + 1) * TOK]
        store_out(g, 0).start()
        corr = -jnp.sum(d.astype(F32) * out.astype(F32), 1, keepdims=True)
        high = corr.astype(BF).astype(F32)
        lane = iota((ROWS, HD), 1)
        corr_cols = jnp.where(lane == 0, high, jnp.where(lane == 1, corr - high, 0.0)).astype(BF)
        dp = dot_nt(jnp.concatenate([v, ones_cols[...]], 1), jnp.concatenate([d, corr_cols], 1))
        ds = (p.astype(F32) * dp).astype(BF)
        dq = (dot(k.T, ds) * (inv * SCALE)).T.astype(BF)
        for a in range(G):
            dqv[:, cols[a]] = dq[a * TOK:(a + 1) * TOK]
        store_out(g, 1).start()
        inv_col = jnp.broadcast_to(inv, (HD, ROWS)).T
        term[g, 1] = dot(p, (d.astype(F32) * inv_col).astype(BF)).astype(BF)
        term[g, 0] = dot(ds, (q.astype(F32) * (inv_col * SCALE)).astype(BF)).astype(BF)
        loop(0, c, lambda j: copy_t(g, j, c).start())
        for n in range(KVH // 2):
            @pl.when(g == 2 * n + 1)
            def _():
                others(nr, r, lambda p: copy_p(n, p, r).start())

    loop(0, KVH, head)

    for n in range(KVH // 2):
        others(nr, r, lambda p: copy_p(n, r, p).wait_recv())
    psum[...] = term[:, :, my_rows, :].astype(F32)

    def add_p(p):
        psum[...] += pterm[p].astype(F32)

    others(nr, r, add_p)
    from_heads = order(False)
    for w in range(2):
        part = jnp.concatenate([psum[g, w] for g in range(KVH)], 0).astype(BF)
        part = dot(from_heads, part).astype(BF)
        for j in range(nc):
            prep[j, w] = part[16 * j:16 * (j + 1)]

    def copy_z(owner, src):
        return pltpu.make_async_remote_copy(
            src_ref=prep.at[owner], dst_ref=pback.at[src],
            send_sem=z_send.at[owner], recv_sem=z_recv.at[src],
            device_id={"ctx": owner}, device_id_type=MESH)

    others(nc, c, lambda p: copy_z(p, c).start())

    def sum_head(g):
        gcol = pl.ds(pl.multiple_of(g * HD, HD), HD)
        kg_ref[:, gcol] = term[g, 0, block_rows(c), :].astype(F32)
        vg_ref[:, gcol] = term[g, 1, block_rows(c), :].astype(F32)

        def add(src):
            copy_t(g, c, src).wait_recv()
            kg_ref[:, gcol] += rterm[src, g, 0].astype(F32)
            vg_ref[:, gcol] += rterm[src, g, 1].astype(F32)

        loop(c + 1, nc, add)

    loop(0, KVH, sum_head)

    others(nc, c, lambda p: copy_z(c, p).wait_recv())
    pkg_ref[...] = prep[c, 0].astype(F32)
    pvg_ref[...] = prep[c, 1].astype(F32)

    def add_z(p):
        pkg_ref[...] += pback[p, 0].astype(F32)
        pvg_ref[...] += pback[p, 1].astype(F32)

    others(nc, c, add_z)

    others(nc, c, lambda p: copy_a(c, p).wait_send())
    for n in range(len(pieces)):
        others(nr, r, lambda p: copy_b(n, r, p).wait_send())
    for n in range(KVH // 2):
        others(nr, r, lambda p: copy_p(n, p, r).wait_send())
    others(nc, c, lambda p: copy_z(p, c).wait_send())

    def finish(g):
        loop(c + 1, nc, lambda p: copy_g(g, c, p).wait_send())
        loop(0, c, lambda j: copy_t(g, j, c).wait_send())
        store_out(g, 0).wait()
        store_out(g, 1).wait()

    loop(0, KVH, finish)


def per_device(
    nr, nc, queries, resp_keys, resp_values, prompt_keys, prompt_values, upstream, lengths, prompt_length
):
    prow = 2 * nc
    key_rows = nr * prow + nc * TOK
    width = KVH * HD
    vmem = pl.BlockSpec(memory_space=pltpu.VMEM)
    smem = pl.BlockSpec(memory_space=pltpu.SMEM)
    hbm = pl.BlockSpec(memory_space=pl.ANY)
    dma = pltpu.SemaphoreType.DMA
    big = jax.ShapeDtypeStruct((TOK, KVH * ROWS), BF)
    grad = jax.ShapeDtypeStruct((TOK, width), F32)
    small = jax.ShapeDtypeStruct((16, HD), F32)
    outs = pl.pallas_call(
        functools.partial(kernel, nr, nc),
        out_shape=(big, big, grad, grad, small, small),
        in_specs=[hbm, hbm, vmem, vmem, vmem, vmem, smem, smem],
        out_specs=[hbm, hbm, vmem, vmem, vmem, vmem],
        scratch_shapes=[
            pltpu.VMEM((TOK, KVH * ROWS), BF),
            pltpu.VMEM((TOK, KVH * ROWS), BF),
            pltpu.VMEM((TOK, KVH * ROWS), BF),
            pltpu.VMEM((TOK, KVH * ROWS), BF),
            pltpu.VMEM((KVH, 2, key_rows, HD), BF),
            pltpu.VMEM((KVH, 2, key_rows, HD), BF),
            pltpu.VMEM((nc, KVH, 2, TOK, HD), BF),
            pltpu.VMEM((key_rows, HD), BF),
            pltpu.VMEM((key_rows, HD), BF),
            pltpu.VMEM((TOK, HD), BF),
            pltpu.VMEM((nc, 2, 16, HD), BF),
            pltpu.VMEM((nc, 2, 16, HD), BF),
            pltpu.VMEM((nr, KVH, 2, prow, HD), BF),
            pltpu.VMEM((KVH, 2, prow, HD), F32),
            pltpu.VMEM((nc, 2, 16, HD), BF),
            dma((2,)), dma((2, KVH)),
            dma((nc,)), dma((nc,)), dma((3, nr)), dma((3, nr)),
            dma((KVH, nc)), dma((KVH, nc)),
            dma((KVH, nc)), dma((KVH, nc)),
            dma((KVH // 2, nr)), dma((KVH // 2, nr)),
            dma((nc,)), dma((nc,)),
        ],
        compiler_params=pltpu.CompilerParams(
            collective_id=0, has_side_effects=True, vmem_limit_bytes=60 * 2**20),
        cost_estimate=pl.CostEstimate(
            flops=12 * KVH * ROWS * key_rows * HD, bytes_accessed=10 * 2**20,
            transcendentals=KVH * ROWS * key_rows),
    )(
        queries[0], upstream[0], resp_keys[0], resp_values[0],
        prompt_keys.reshape(16, HD), prompt_values.reshape(16, HD), lengths, prompt_length,
    )
    attended, query_grads, key_grads, value_grads, pkg, pvg = outs
    return (
        attended[None], query_grads[None], key_grads[None], value_grads[None],
        pkg.reshape(2, width), pvg.reshape(2, width),
    )


def solution(mesh):
    tokens = P("resp", "ctx", None)
    rows = P(("resp", "ctx"), None)
    return jax.shard_map(
        functools.partial(per_device, mesh.shape["resp"], mesh.shape["ctx"]),
        mesh=mesh,
        in_specs=(tokens, tokens, tokens, rows, rows, tokens, P("resp"), P()),
        out_specs=(tokens, tokens, tokens, tokens, rows, rows),
        check_vma=False,
    )
```

```python
import functools

import jax
import jax.numpy as jnp
from jax import lax
from jax.experimental import pallas as pl
from jax.experimental.pallas import tpu as pltpu
from jax.sharding import PartitionSpec as P

HD = 128
KVH = 8
G = 8
ROWS = G * HD
TOK = 128
SCALE = HD**-0.5
LOG2E = 1.4426950408889634
HIDE = -1e30
NT = (((1,), (1,)), ((), ()))
F32 = jnp.float32
BF = jnp.bfloat16
MESH = pl.DeviceIdType.MESH

PROMPT_IN = ((0, 1), (1, 2), (3, 5))
PROMPT_OUT = ((0, 4), (4, 3), (7, 1))
GATHER = ((0, 1), (1, 1), (2, 2), (4, 2), (6, 2))
TERMS = tuple((g, 1) for g in range(8))


def iota(shape, axis):
    return lax.broadcasted_iota(jnp.int32, shape, axis)


def dot(a, b):
    return jnp.dot(a, b, preferred_element_type=F32)


def dot_nt(a, b):
    return lax.dot_general(a, b, NT, preferred_element_type=F32)


def kernel(
    nr, nc,
    q_hbm, d_hbm, k_ref, v_ref, pk_ref, pv_ref, len_ref, plen_ref,
    out_hbm, dq_hbm, kg_ref, vg_ref, pkg_ref, pvg_ref,
    qv, dv, ov, dqv, kv, term, rterm, hidden_cols, ones_cols, causal_cols,
    pown, prep, pterm, psum, xsend, xrecv, pback,
    in_sem, out_sem, x_sem,
    a_send, a_recv, b_send, b_recv, g_send, g_recv,
    t_send, t_recv, p_send, p_recv, z_send, z_recv,
):
    prow = 2 * nc
    prompt = nr * prow
    key_rows = prompt + nc * TOK
    r = lax.axis_index("resp")
    c = lax.axis_index("ctx")
    nm = nr // 2
    half = lax.rem(r // 2, 2)
    m = (r // 4) * 2 + lax.rem(r, 2)
    partner = r + 2 - 4 * half

    def resp_of(pair):
        return (pair // 2) * 4 + 2 * half + lax.rem(pair, 2)

    load_q = pltpu.make_async_copy(q_hbm, qv, in_sem.at[0])
    load_d = pltpu.make_async_copy(d_hbm, dv, in_sem.at[1])
    load_q.start()
    load_d.start()

    barrier = pltpu.get_barrier_semaphore()

    def others(n, me, body):
        def step(i, carry):
            body(lax.rem(me + i, n))
            return carry

        lax.fori_loop(1, n, step, 0)

    others(nc, c, lambda p: pl.semaphore_signal(barrier, inc=1, device_id={"ctx": p}, device_id_type=MESH))
    others(nm, m, lambda p: pl.semaphore_signal(
        barrier, inc=1, device_id={"resp": resp_of(p)}, device_id_type=MESH))
    pl.semaphore_signal(barrier, inc=1, device_id={"resp": partner}, device_id_type=MESH)

    def block_rows(j):
        return pl.ds(pl.multiple_of(prompt + j * TOK, TOK), TOK)

    for w, ref in enumerate((pk_ref, pv_ref)):
        wide = ref[...].astype(F32)
        rows = [wide[:, g * HD:(g + 1) * HD] for g in range(KVH)]
        pown[half, c, w] = jnp.concatenate(rows, 0).astype(BF)
    for g in range(KVH):
        kv[g, 0, block_rows(c), :] = k_ref[:, g * HD:(g + 1) * HD]
        kv[g, 1, block_rows(c), :] = v_ref[:, g * HD:(g + 1) * HD]

    pl.semaphore_wait(barrier, nc - 1 + nm)

    def copy_a(slot, peer):
        return pltpu.make_async_remote_copy(
            src_ref=pown.at[half, slot], dst_ref=pown.at[half, slot],
            send_sem=a_send.at[peer], recv_sem=a_recv.at[slot],
            device_id={"ctx": peer}, device_id_type=MESH)

    others(nc, c, lambda p: copy_a(c, p).start())

    def copy_g(n, slot, peer):
        g0, count = GATHER[n]
        part = kv.at[pl.ds(g0, count), :, block_rows(slot), :]
        return pltpu.make_async_remote_copy(
            src_ref=part, dst_ref=part,
            send_sem=g_send.at[n, peer], recv_sem=g_recv.at[n, slot],
            device_id={"ctx": peer}, device_id_type=MESH)

    def loop(lo, hi, body):
        def step(i, carry):
            body(i)
            return carry

        lax.fori_loop(lo, hi, step, 0)

    def gather(n):
        loop(c + 1, nc, lambda p: copy_g(n, c, p).start())

    gather(0)
    gather(1)
    gather(2)

    def clear(j):
        def one(g):
            kv[g, 0, block_rows(j), :] = jnp.zeros((TOK, HD), BF)
            kv[g, 1, block_rows(j), :] = jnp.zeros((TOK, HD), BF)
        loop(0, KVH, one)

    loop(c + 1, nc, clear)

    row = iota((key_rows, HD), 0)
    col = iota((key_rows, HD), 1)
    slot, within = row // prow, lax.rem(row, prow)
    place = ((slot // 4) * 4 + lax.rem(slot, 2) * 2 + lax.rem(slot // 2, 2)) * prow + within
    gone = ((row < prompt) & (place >= plen_ref[0])) | (row >= prompt + (c + 1) * TOK)
    diagonal = (row - (prompt + c * TOK) == col) & (col > 0)
    hidden_cols[...] = jnp.where(diagonal, 1.0, jnp.where(gone & (col == 0), HIDE, 0.0)).astype(BF)
    ones_cols[...] = jnp.where(col < 2, 1.0, 0.0).astype(BF)
    tok = iota((TOK, HD), 0)
    key = iota((TOK, HD), 1)
    causal_cols[...] = jnp.where(key == 0, 1.0, jnp.where(key > tok, HIDE, 0.0)).astype(BF)
    live = c * TOK + tok < len_ref[0]
    live_lane = jnp.where(c * TOK + iota((1, TOK), 1) < len_ref[0], 1.0, 0.0)

    n16 = 16 * nc

    def order(to_heads):
        a = iota((n16, n16), 0)
        b = iota((n16, n16), 1)
        if not to_heads:
            a, b = b, a
        head, rest = a // prow, lax.rem(a, prow)
        return jnp.where((rest // 2) * 16 + head * 2 + lax.rem(rest, 2) == b, 1.0, 0.0).astype(BF)

    def copy_x(which, src, dst):
        return pltpu.make_async_remote_copy(
            src_ref=src, dst_ref=dst, send_sem=x_sem.at[which, 0], recv_sem=x_sem.at[which, 1],
            device_id={"resp": partner}, device_id_type=MESH)

    to_heads = order(True)
    others(nc, c, lambda p: copy_a(p, p).wait_recv())
    swap = copy_x(0, pown.at[half], pown.at[half])
    swap.start()
    swap.wait_recv()

    def pair_rows(pair, h=0, count=2):
        return pl.ds(pl.multiple_of((2 * pair + h) * prow, prow), count * prow)

    for h in range(2):
        for w in range(2):
            got = jnp.concatenate([pown[h, j, w] for j in range(nc)], 0)
            mine = dot(to_heads, got).astype(BF)
            for g in range(KVH):
                kv[g, w, pair_rows(m, h, 1), :] = mine[g * prow:(g + 1) * prow]

    def copy_b(n, slot, peer):
        g0, count = PROMPT_IN[n]
        part = kv.at[pl.ds(g0, count), :, pair_rows(slot), :]
        return pltpu.make_async_remote_copy(
            src_ref=part, dst_ref=part,
            send_sem=b_send.at[n, peer], recv_sem=b_recv.at[n, slot],
            device_id={"resp": resp_of(peer)}, device_id_type=MESH)

    for n in range(len(PROMPT_IN)):
        others(nm, m, lambda p: copy_b(n, m, p).start())

    load_q.wait()
    load_d.wait()

    def copy_t(n, block, src):
        g0, count = TERMS[n]
        return pltpu.make_async_remote_copy(
            src_ref=term.at[pl.ds(g0, count), :, block_rows(block), :],
            dst_ref=rterm.at[src, pl.ds(g0, count)],
            send_sem=t_send.at[n, block], recv_sem=t_recv.at[n, src],
            device_id={"ctx": block}, device_id_type=MESH)

    def copy_p(n, owner, src):
        g0, count = PROMPT_OUT[n]
        return pltpu.make_async_remote_copy(
            src_ref=term.at[pl.ds(g0, count), :, pair_rows(owner), :],
            dst_ref=pterm.at[src, pl.ds(g0, count)],
            send_sem=p_send.at[n, owner], recv_sem=p_recv.at[n, src],
            device_id={"resp": resp_of(owner)}, device_id_type=MESH)

    def store_out(g, which):
        cols = pl.ds(pl.multiple_of(g * ROWS, ROWS), ROWS)
        src, dst = ((ov, out_hbm), (dqv, dq_hbm))[which]
        return pltpu.make_async_copy(src.at[:, cols], dst.at[:, cols], out_sem.at[which, g])

    def head(g):
        for n, (g0, _) in enumerate(PROMPT_IN):
            @pl.when(g == g0)
            def _():
                others(nm, m, lambda p: copy_b(n, p, p).wait_recv())
        for n, (g0, _) in enumerate(GATHER):
            @pl.when(g == g0)
            def _():
                loop(0, c, lambda j: copy_g(n, j, j).wait_recv())
            if n >= 3:
                @pl.when(g == g0 - 4)
                def _():
                    gather(n)

        cols = [pl.ds(pl.multiple_of(g * ROWS + a * HD, HD), HD) for a in range(G)]
        k = kv[g, 0]
        v = kv[g, 1]
        q = jnp.concatenate([qv[:, x] for x in cols], 0)
        d = jnp.concatenate([jnp.where(live, dv[:, x], jnp.zeros((), BF)) for x in cols], 0)
        limit = jnp.concatenate([causal_cols[...]] * G, 0)
        s = dot_nt(jnp.concatenate([k, hidden_cols[...]], 1), jnp.concatenate([q, limit], 1))
        top = jnp.max(s, 0, keepdims=True)
        p = jnp.exp2((s - top) * (SCALE * LOG2E))
        inv = 1.0 / jnp.sum(p, 0, keepdims=True)
        p = p.astype(BF)
        out = dot(v.T, p) * (inv * jnp.concatenate([live_lane] * G, 1))
        out = out.T.astype(BF)
        for a in range(G):
            ov[:, cols[a]] = out[a * TOK:(a + 1) * TOK]
        store_out(g, 0).start()
        corr = -jnp.sum(d.astype(F32) * out.astype(F32), 1, keepdims=True)
        high = corr.astype(BF).astype(F32)
        lane = iota((ROWS, HD), 1)
        corr_cols = jnp.where(lane == 0, high, jnp.where(lane == 1, corr - high, 0.0)).astype(BF)
        dp = dot_nt(jnp.concatenate([v, ones_cols[...]], 1), jnp.concatenate([d, corr_cols], 1))
        ds = (p.astype(F32) * dp).astype(BF)
        dq = (dot(k.T, ds) * (inv * SCALE)).T.astype(BF)
        for a in range(G):
            dqv[:, cols[a]] = dq[a * TOK:(a + 1) * TOK]
        store_out(g, 1).start()
        inv_col = jnp.broadcast_to(inv, (HD, ROWS)).T
        term[g, 1] = dot(p, (d.astype(F32) * inv_col).astype(BF)).astype(BF)
        term[g, 0] = dot(ds, (q.astype(F32) * (inv_col * SCALE)).astype(BF)).astype(BF)
        for n, (g0, count) in enumerate(TERMS):
            @pl.when(g == g0 + count - 1)
            def _():
                loop(0, c, lambda j: copy_t(n, j, c).start())
        for n, (g0, count) in enumerate(PROMPT_OUT):
            @pl.when(g == g0 + count - 1)
            def _():
                others(nm, m, lambda p: copy_p(n, p, m).start())

    loop(0, KVH, head)

    for n in range(len(PROMPT_OUT)):
        others(nm, m, lambda p: copy_p(n, m, p).wait_recv())
    for h in range(2):
        psum[h] = term[:, :, pair_rows(m, h, 1), :].astype(F32)

    def add_p(p):
        for h in range(2):
            psum[h] += pterm[p, :, :, h * prow:(h + 1) * prow, :].astype(F32)

    others(nm, m, add_p)
    xsend[...] = psum[1 - half].astype(BF)
    swap_back = copy_x(1, xsend, xrecv)
    swap_back.start()
    swap_back.wait_recv()
    psum[half] += xrecv[...].astype(F32)
    from_heads = order(False)
    for w in range(2):
        part = jnp.concatenate([psum[half, g, w] for g in range(KVH)], 0).astype(BF)
        part = dot(from_heads, part).astype(BF)
        for j in range(nc):
            prep[j, w] = part[16 * j:16 * (j + 1)]

    def copy_z(owner, src):
        return pltpu.make_async_remote_copy(
            src_ref=prep.at[owner], dst_ref=pback.at[src],
            send_sem=z_send.at[owner], recv_sem=z_recv.at[src],
            device_id={"ctx": owner}, device_id_type=MESH)

    others(nc, c, lambda p: copy_z(p, c).start())

    for n, (g0, count) in enumerate(TERMS):
        loop(c + 1, nc, lambda src: copy_t(n, c, src).wait_recv())
        for g in range(g0, g0 + count):
            for w, ref in enumerate((kg_ref, vg_ref)):
                ref[:, g * HD:(g + 1) * HD] = lax.fori_loop(
                    c + 1, nc, lambda src, total: total + rterm[src, g, w].astype(F32),
                    term[g, w, block_rows(c), :].astype(F32))

    others(nc, c, lambda p: copy_z(c, p).wait_recv())
    for w, ref in enumerate((pkg_ref, pvg_ref)):
        total = prep[c, w].astype(F32)
        for i in range(1, nc):
            total += pback[lax.rem(c + i, nc), w].astype(F32)
        for g in range(KVH):
            ref[:, g * HD:(g + 1) * HD] = total[2 * g:2 * g + 2]

    others(nc, c, lambda p: copy_a(c, p).wait_send())
    swap.wait_send()
    swap_back.wait_send()
    for n in range(len(PROMPT_IN)):
        others(nm, m, lambda p: copy_b(n, m, p).wait_send())
    for n in range(len(PROMPT_OUT)):
        others(nm, m, lambda p: copy_p(n, p, m).wait_send())
    others(nc, c, lambda p: copy_z(p, c).wait_send())
    for n in range(len(GATHER)):
        loop(c + 1, nc, lambda p: copy_g(n, c, p).wait_send())
    for n in range(len(TERMS)):
        loop(0, c, lambda j: copy_t(n, j, c).wait_send())

    def finish(g):
        store_out(g, 0).wait()
        store_out(g, 1).wait()

    loop(0, KVH, finish)


def per_device(
    nr, nc, queries, resp_keys, resp_values, prompt_keys, prompt_values, upstream, lengths, prompt_length
):
    prow = 2 * nc
    key_rows = nr * prow + nc * TOK
    width = KVH * HD
    vmem = pl.BlockSpec(memory_space=pltpu.VMEM)
    smem = pl.BlockSpec(memory_space=pltpu.SMEM)
    hbm = pl.BlockSpec(memory_space=pl.ANY)
    dma = pltpu.SemaphoreType.DMA
    big = jax.ShapeDtypeStruct((TOK, KVH * ROWS), BF)
    grad = jax.ShapeDtypeStruct((TOK, width), F32)
    small = jax.ShapeDtypeStruct((2, width), F32)
    outs = pl.pallas_call(
        functools.partial(kernel, nr, nc),
        out_shape=(big, big, grad, grad, small, small),
        in_specs=[hbm, hbm, vmem, vmem, vmem, vmem, smem, smem],
        out_specs=[hbm, hbm, vmem, vmem, vmem, vmem],
        scratch_shapes=[
            pltpu.VMEM((TOK, KVH * ROWS), BF),
            pltpu.VMEM((TOK, KVH * ROWS), BF),
            pltpu.VMEM((TOK, KVH * ROWS), BF),
            pltpu.VMEM((TOK, KVH * ROWS), BF),
            pltpu.VMEM((KVH, 2, key_rows, HD), BF),
            pltpu.VMEM((KVH, 2, key_rows, HD), BF),
            pltpu.VMEM((nc, KVH, 2, TOK, HD), BF),
            pltpu.VMEM((key_rows, HD), BF),
            pltpu.VMEM((key_rows, HD), BF),
            pltpu.VMEM((TOK, HD), BF),
            pltpu.VMEM((2, nc, 2, 16, HD), BF),
            pltpu.VMEM((nc, 2, 16, HD), BF),
            pltpu.VMEM((nr // 2, KVH, 2, 2 * prow, HD), BF),
            pltpu.VMEM((2, KVH, 2, prow, HD), F32),
            pltpu.VMEM((KVH, 2, prow, HD), BF),
            pltpu.VMEM((KVH, 2, prow, HD), BF),
            pltpu.VMEM((nc, 2, 16, HD), BF),
            dma((2,)), dma((2, KVH)), dma((2, 2)),
            dma((nc,)), dma((nc,)),
            dma((len(PROMPT_IN), nr // 2)), dma((len(PROMPT_IN), nr // 2)),
            dma((len(GATHER), nc)), dma((len(GATHER), nc)),
            dma((len(TERMS), nc)), dma((len(TERMS), nc)),
            dma((len(PROMPT_OUT), nr // 2)), dma((len(PROMPT_OUT), nr // 2)),
            dma((nc,)), dma((nc,)),
        ],
        compiler_params=pltpu.CompilerParams(
            collective_id=0, has_side_effects=True, vmem_limit_bytes=60 * 2**20),
        cost_estimate=pl.CostEstimate(
            flops=12 * KVH * ROWS * key_rows * HD, bytes_accessed=10 * 2**20,
            transcendentals=KVH * ROWS * key_rows),
    )(
        queries[0], upstream[0], resp_keys[0], resp_values[0],
        prompt_keys, prompt_values, lengths, prompt_length,
    )
    attended, query_grads, key_grads, value_grads, pkg, pvg = outs
    return (
        attended[None], query_grads[None], key_grads[None], value_grads[None],
        pkg, pvg,
    )


def solution(mesh):
    tokens = P("resp", "ctx", None)
    rows = P(("resp", "ctx"), None)
    return jax.shard_map(
        functools.partial(per_device, mesh.shape["resp"], mesh.shape["ctx"]),
        mesh=mesh,
        in_specs=(tokens, tokens, tokens, rows, rows, tokens, P("resp"), P()),
        out_specs=(tokens, tokens, tokens, tokens, rows, rows),
        check_vma=False,
    )
```

```python
import functools

import jax
import jax.numpy as jnp
from jax import lax
from jax.experimental import pallas as pl
from jax.experimental.pallas import tpu as pltpu
from jax.sharding import PartitionSpec as P

HD = 128
KVH = 8
G = 8
ROWS = G * HD
TOK = 128
SCALE = HD**-0.5
LOG2E = 1.4426950408889634
HIDE = -1e30
NT = (((1,), (1,)), ((), ()))
F32 = jnp.float32
BF = jnp.bfloat16
MESH = pl.DeviceIdType.MESH

PROMPT_IN = ((0, 1), (1, 2), (3, 5))
PROMPT_OUT = ((0, 4), (4, 3), (7, 1))
GATHER = tuple((g, 1) for g in range(8))
TERMS = tuple((g, 1) for g in range(8))


def iota(shape, axis):
    return lax.broadcasted_iota(jnp.int32, shape, axis)


def dot(a, b):
    return jnp.dot(a, b, preferred_element_type=F32)


def dot_nt(a, b):
    return lax.dot_general(a, b, NT, preferred_element_type=F32)


def kernel(
    nr, nc,
    q_hbm, d_hbm, k_hbm, v_hbm, pk_hbm, pv_hbm, len_ref, plen_ref,
    ov, dqv, kg_ref, vg_ref, pkg_ref, pvg_ref,
    qv, dv, k_ref, v_ref, pk_ref, pv_ref, kv, term, rterm, hidden_cols, causal_cols,
    pown, prep, pterm, psum, xsend, xrecv, pback,
    in_sem, x_sem,
    a_send, a_recv, b_send, b_recv, g_send, g_recv,
    t_send, t_recv, p_send, p_recv, z_send, z_recv,
):
    prow = 2 * nc
    prompt = nr * prow
    key_rows = prompt + nc * TOK
    r = lax.axis_index("resp")
    c = lax.axis_index("ctx")
    nm = nr // 2
    half = lax.rem(r // 2, 2)
    m = (r // 4) * 2 + lax.rem(r, 2)
    partner = r + 2 - 4 * half

    def resp_of(pair):
        return (pair // 2) * 4 + 2 * half + lax.rem(pair, 2)

    load_q = pltpu.make_async_copy(q_hbm, qv, in_sem.at[0])
    load_d = pltpu.make_async_copy(d_hbm, dv, in_sem.at[1])
    loads = [
        pltpu.make_async_copy(src, dst, in_sem.at[2 + n])
        for n, (src, dst) in enumerate(((pk_hbm, pk_ref), (pv_hbm, pv_ref), (k_hbm, k_ref), (v_hbm, v_ref)))
    ]
    for load in loads:
        load.start()
    load_q.start()
    load_d.start()

    barrier = pltpu.get_barrier_semaphore()

    def others(n, me, body):
        def step(i, carry):
            body(lax.rem(me + i, n))
            return carry

        lax.fori_loop(1, n, step, 0)

    others(nc, c, lambda p: pl.semaphore_signal(barrier, inc=1, device_id={"ctx": p}, device_id_type=MESH))
    others(nm, m, lambda p: pl.semaphore_signal(
        barrier, inc=1, device_id={"resp": resp_of(p)}, device_id_type=MESH))
    pl.semaphore_signal(barrier, inc=1, device_id={"resp": partner}, device_id_type=MESH)

    def block_rows(j):
        return pl.ds(pl.multiple_of(prompt + j * TOK, TOK), TOK)

    for load in loads:
        load.wait()
    for w, ref in enumerate((pk_ref, pv_ref)):
        wide = ref[...].astype(F32)
        rows = [wide[:, g * HD:(g + 1) * HD] for g in range(KVH)]
        pown[half, c, w] = jnp.concatenate(rows, 0).astype(BF)
    for g in range(KVH):
        kv[g, 0, block_rows(c), :] = k_ref[:, g * HD:(g + 1) * HD]
        kv[g, 1, block_rows(c), :] = v_ref[:, g * HD:(g + 1) * HD]

    pl.semaphore_wait(barrier, nc - 1 + nm)

    def copy_a(slot, peer):
        return pltpu.make_async_remote_copy(
            src_ref=pown.at[half, slot], dst_ref=pown.at[half, slot],
            send_sem=a_send.at[peer], recv_sem=a_recv.at[slot],
            device_id={"ctx": peer}, device_id_type=MESH)

    others(nc, c, lambda p: copy_a(c, p).start())

    def copy_g(n, slot, peer):
        g0, count = GATHER[n]
        part = kv.at[pl.ds(g0, count), :, block_rows(slot), :]
        return pltpu.make_async_remote_copy(
            src_ref=part, dst_ref=part,
            send_sem=g_send.at[n, peer], recv_sem=g_recv.at[n, slot],
            device_id={"ctx": peer}, device_id_type=MESH)

    def loop(lo, hi, body):
        def step(i, carry):
            body(i)
            return carry

        lax.fori_loop(lo, hi, step, 0)

    def gather(n):
        loop(0, nc - 1 - c, lambda i: copy_g(n, c, nc - 1 - i).start())


    def clear(j):
        def one(g):
            kv[g, 0, block_rows(j), :] = jnp.zeros((TOK, HD), BF)
            kv[g, 1, block_rows(j), :] = jnp.zeros((TOK, HD), BF)
        loop(0, KVH, one)

    loop(c + 1, nc, clear)

    row = iota((key_rows, HD), 0)
    col = iota((key_rows, HD), 1)
    slot, within = row // prow, lax.rem(row, prow)
    place = ((slot // 4) * 4 + lax.rem(slot, 2) * 2 + lax.rem(slot // 2, 2)) * prow + within
    gone = ((row < prompt) & (place >= plen_ref[0])) | (row >= prompt + (c + 1) * TOK)
    diagonal = (row - (prompt + c * TOK) == col) & (col > 0)
    hidden_cols[...] = jnp.where(diagonal, 1.0, jnp.where(gone & (col == 0), HIDE, 0.0)).astype(BF)
    tok = iota((TOK, HD), 0)
    key = iota((TOK, HD), 1)
    causal_cols[...] = jnp.where(key == 0, 1.0, jnp.where(key > tok, HIDE, 0.0)).astype(BF)
    live = c * TOK + tok < len_ref[0]
    live_lane = jnp.where(c * TOK + iota((1, TOK), 1) < len_ref[0], 1.0, 0.0)

    n16 = 16 * nc

    def order(to_heads):
        a = iota((n16, n16), 0)
        b = iota((n16, n16), 1)
        if not to_heads:
            a, b = b, a
        head, rest = a // prow, lax.rem(a, prow)
        return jnp.where((rest // 2) * 16 + head * 2 + lax.rem(rest, 2) == b, 1.0, 0.0).astype(BF)

    def copy_x(which, src, dst):
        return pltpu.make_async_remote_copy(
            src_ref=src, dst_ref=dst, send_sem=x_sem.at[which, 0], recv_sem=x_sem.at[which, 1],
            device_id={"resp": partner}, device_id_type=MESH)

    to_heads = order(True)
    others(nc, c, lambda p: copy_a(p, p).wait_recv())
    gather(0)
    swap = copy_x(0, pown.at[half], pown.at[half])
    swap.start()
    swap.wait_recv()
    gather(1)

    def pair_rows(pair, h=0, count=2):
        return pl.ds(pl.multiple_of((2 * pair + h) * prow, prow), count * prow)

    for h in range(2):
        for w in range(2):
            got = jnp.concatenate([pown[h, j, w] for j in range(nc)], 0)
            mine = dot(to_heads, got).astype(BF)
            for g in range(KVH):
                kv[g, w, pair_rows(m, h, 1), :] = mine[g * prow:(g + 1) * prow]

    def copy_b(n, slot, peer):
        g0, count = PROMPT_IN[n]
        part = kv.at[pl.ds(g0, count), :, pair_rows(slot), :]
        return pltpu.make_async_remote_copy(
            src_ref=part, dst_ref=part,
            send_sem=b_send.at[n, peer], recv_sem=b_recv.at[n, slot],
            device_id={"resp": resp_of(peer)}, device_id_type=MESH)

    def prompt_in(n):
        others(nm, m, lambda p: copy_b(n, m, p).start())

    prompt_in(0)

    load_q.wait()
    load_d.wait()

    def copy_t(n, block, src):
        g0, count = TERMS[n]
        return pltpu.make_async_remote_copy(
            src_ref=term.at[pl.ds(g0, count), :, block_rows(block), :],
            dst_ref=rterm.at[src, pl.ds(g0, count)],
            send_sem=t_send.at[n, block], recv_sem=t_recv.at[n, src],
            device_id={"ctx": block}, device_id_type=MESH)

    def copy_p(n, owner, src):
        g0, count = PROMPT_OUT[n]
        return pltpu.make_async_remote_copy(
            src_ref=term.at[pl.ds(g0, count), :, pair_rows(owner), :],
            dst_ref=pterm.at[src, pl.ds(g0, count)],
            send_sem=p_send.at[n, owner], recv_sem=p_recv.at[n, src],
            device_id={"resp": resp_of(owner)}, device_id_type=MESH)

    def sum_prompt(n):
        g0, count = PROMPT_OUT[n]
        heads = pl.ds(g0, count)
        others(nm, m, lambda p: copy_p(n, m, p).wait_recv())
        for h in range(2):
            psum[h, heads] = term[heads, :, pair_rows(m, h, 1), :].astype(F32)

        def add(p):
            for h in range(2):
                psum[h, heads] += pterm[p, heads, :, h * prow:(h + 1) * prow, :].astype(F32)

        others(nm, m, add)

    def head(g):
        for n, (g0, _) in enumerate(PROMPT_IN):
            @pl.when(g == g0)
            def _():
                others(nm, m, lambda p: copy_b(n, p, p).wait_recv())
        for n in (1, 2):
            @pl.when(g == n - 1)
            def _():
                prompt_in(n)

        for n, (g0, _) in enumerate(GATHER):
            @pl.when(g == g0)
            def _():
                loop(0, c, lambda j: copy_g(n, j, j).wait_recv())

        for n in range(1, KVH):
            @pl.when((g == n - 2) & (n >= 2))
            def _():
                gather(n)

        cols = [pl.ds(pl.multiple_of(g * ROWS + a * HD, HD), HD) for a in range(G)]
        k = kv[g, 0]
        v = kv[g, 1]
        q = jnp.concatenate([qv[:, x] for x in cols], 0)
        d = jnp.concatenate([jnp.where(live, dv[:, x], jnp.zeros((), BF)) for x in cols], 0)
        limit = jnp.concatenate([causal_cols[...]] * G, 0)
        s = dot_nt(jnp.concatenate([k, hidden_cols[...]], 1), jnp.concatenate([q, limit], 1))
        dp = dot_nt(v, d)
        top = jnp.max(s, 0, keepdims=True)
        p = jnp.exp2((s - top) * (SCALE * LOG2E))
        inv = 1.0 / jnp.sum(p, 0, keepdims=True)
        p = p.astype(BF)
        out = (dot(v.T, p) * (inv * jnp.concatenate([live_lane] * G, 1))).astype(BF)
        corr = jnp.sum(d.T.astype(F32) * out.astype(F32), 0, keepdims=True)
        out = out.T
        for a in range(G):
            ov[:, cols[a]] = out[a * TOK:(a + 1) * TOK]
        ds = p * (dp - corr).astype(BF)
        dq = (dot(k.T, ds) * (inv * SCALE)).T.astype(BF)
        for a in range(G):
            dqv[:, cols[a]] = dq[a * TOK:(a + 1) * TOK]
        inv_col = jnp.broadcast_to(inv, (HD, ROWS)).T
        term[g, 1] = dot(p, (d.astype(F32) * inv_col).astype(BF)).astype(BF)
        term[g, 0] = dot(ds, (q.astype(F32) * (inv_col * SCALE)).astype(BF)).astype(BF)
        for n, (g0, count) in enumerate(TERMS):
            @pl.when(g == g0 + count - 1)
            def _():
                loop(0, c, lambda j: copy_t(n, j, c).start())
        for n, (g0, count) in enumerate(PROMPT_OUT):
            @pl.when(g == g0 + count - 1)
            def _():
                others(nm, m, lambda p: copy_p(n, p, m).start())

        @pl.when(g == 6)
        def _():
            sum_prompt(0)

    loop(0, KVH, head)

    sum_prompt(1)
    sum_prompt(2)
    xsend[...] = psum[1 - half].astype(BF)
    swap_back = copy_x(1, xsend, xrecv)
    swap_back.start()
    swap_back.wait_recv()
    psum[half] += xrecv[...].astype(F32)
    from_heads = order(False)
    for w in range(2):
        part = jnp.concatenate([psum[half, g, w] for g in range(KVH)], 0).astype(BF)
        part = dot(from_heads, part).astype(BF)
        for j in range(nc):
            prep[j, w] = part[16 * j:16 * (j + 1)]

    def copy_z(owner, src):
        return pltpu.make_async_remote_copy(
            src_ref=prep.at[owner], dst_ref=pback.at[src],
            send_sem=z_send.at[owner], recv_sem=z_recv.at[src],
            device_id={"ctx": owner}, device_id_type=MESH)

    others(nc, c, lambda p: copy_z(p, c).start())

    for n, (g0, count) in enumerate(TERMS):
        loop(c + 1, nc, lambda src: copy_t(n, c, src).wait_recv())
        for g in range(g0, g0 + count):
            for w, ref in enumerate((kg_ref, vg_ref)):
                ref[:, g * HD:(g + 1) * HD] = lax.fori_loop(
                    c + 1, nc, lambda src, total: total + rterm[src, g, w].astype(F32),
                    term[g, w, block_rows(c), :].astype(F32))

    others(nc, c, lambda p: copy_z(c, p).wait_recv())
    for w, ref in enumerate((pkg_ref, pvg_ref)):
        total = prep[c, w].astype(F32)
        for i in range(1, nc):
            total += pback[lax.rem(c + i, nc), w].astype(F32)
        for g in range(KVH):
            ref[:, g * HD:(g + 1) * HD] = total[2 * g:2 * g + 2]

    others(nc, c, lambda p: copy_a(c, p).wait_send())
    swap.wait_send()
    swap_back.wait_send()
    for n in range(len(PROMPT_IN)):
        others(nm, m, lambda p: copy_b(n, m, p).wait_send())
    for n in range(len(PROMPT_OUT)):
        others(nm, m, lambda p: copy_p(n, p, m).wait_send())
    others(nc, c, lambda p: copy_z(p, c).wait_send())
    for n in range(len(GATHER)):
        loop(c + 1, nc, lambda p: copy_g(n, c, p).wait_send())
    for n in range(len(TERMS)):
        loop(0, c, lambda j: copy_t(n, j, c).wait_send())


def per_device(
    nr, nc, queries, resp_keys, resp_values, prompt_keys, prompt_values, upstream, lengths, prompt_length
):
    prow = 2 * nc
    key_rows = nr * prow + nc * TOK
    width = KVH * HD
    vmem = pl.BlockSpec(memory_space=pltpu.VMEM)
    smem = pl.BlockSpec(memory_space=pltpu.SMEM)
    hbm = pl.BlockSpec(memory_space=pltpu.HBM)
    dma = pltpu.SemaphoreType.DMA
    big = jax.ShapeDtypeStruct((TOK, KVH * ROWS), BF)
    grad = jax.ShapeDtypeStruct((TOK, width), F32)
    small = jax.ShapeDtypeStruct((2, width), F32)
    outs = pl.pallas_call(
        functools.partial(kernel, nr, nc),
        out_shape=(big, big, grad, grad, small, small),
        in_specs=[hbm] * 6 + [smem, smem],
        out_specs=[vmem] * 6,
        scratch_shapes=[
            pltpu.VMEM((TOK, KVH * ROWS), BF),
            pltpu.VMEM((TOK, KVH * ROWS), BF),
            pltpu.VMEM((TOK, width), BF),
            pltpu.VMEM((TOK, width), BF),
            pltpu.VMEM((2, width), BF),
            pltpu.VMEM((2, width), BF),
            pltpu.VMEM((KVH, 2, key_rows, HD), BF),
            pltpu.VMEM((KVH, 2, key_rows, HD), BF),
            pltpu.VMEM((nc, KVH, 2, TOK, HD), BF),
            pltpu.VMEM((key_rows, HD), BF),
            pltpu.VMEM((TOK, HD), BF),
            pltpu.VMEM((2, nc, 2, 16, HD), BF),
            pltpu.VMEM((nc, 2, 16, HD), BF),
            pltpu.VMEM((nr // 2, KVH, 2, 2 * prow, HD), BF),
            pltpu.VMEM((2, KVH, 2, prow, HD), F32),
            pltpu.VMEM((KVH, 2, prow, HD), BF),
            pltpu.VMEM((KVH, 2, prow, HD), BF),
            pltpu.VMEM((nc, 2, 16, HD), BF),
            dma((6,)), dma((2, 2)),
            dma((nc,)), dma((nc,)),
            dma((len(PROMPT_IN), nr // 2)), dma((len(PROMPT_IN), nr // 2)),
            dma((len(GATHER), nc)), dma((len(GATHER), nc)),
            dma((len(TERMS), nc)), dma((len(TERMS), nc)),
            dma((len(PROMPT_OUT), nr // 2)), dma((len(PROMPT_OUT), nr // 2)),
            dma((nc,)), dma((nc,)),
        ],
        compiler_params=pltpu.CompilerParams(
            collective_id=0, has_side_effects=True, vmem_limit_bytes=58 * 2**20),
        cost_estimate=pl.CostEstimate(
            flops=12 * KVH * ROWS * key_rows * HD, bytes_accessed=10 * 2**20,
            transcendentals=KVH * ROWS * key_rows),
    )(
        queries[0], upstream[0], resp_keys[0], resp_values[0],
        prompt_keys, prompt_values, lengths, prompt_length,
    )
    attended, query_grads, key_grads, value_grads, pkg, pvg = outs
    return (
        attended[None], query_grads[None], key_grads[None], value_grads[None],
        pkg, pvg,
    )


def solution(mesh):
    tokens = P("resp", "ctx", None)
    rows = P(("resp", "ctx"), None)
    return jax.shard_map(
        functools.partial(per_device, mesh.shape["resp"], mesh.shape["ctx"]),
        mesh=mesh,
        in_specs=(tokens, tokens, tokens, rows, rows, tokens, P("resp"), P()),
        out_specs=(tokens, tokens, tokens, tokens, rows, rows),
        check_vma=False,
    )
```

```python
import functools

import jax
import jax.numpy as jnp
from jax import lax
from jax.experimental import pallas as pl
from jax.experimental.pallas import tpu as pltpu
from jax.sharding import PartitionSpec as P

HD = 128
KVH = 8
G = 8
ROWS = G * HD
TOK = 128
SCALE = HD**-0.5
LOG2E = 1.4426950408889634
HIDE = -1e30
NT = (((1,), (1,)), ((), ()))
F32 = jnp.float32
BF = jnp.bfloat16
MESH = pl.DeviceIdType.MESH

PROMPT_IN = ((0, 1), (1, 2), (3, 5))
PROMPT_OUT = ((0, 4), (4, 3), (7, 1))


def iota(shape, axis):
    return lax.broadcasted_iota(jnp.int32, shape, axis)


def dot(a, b):
    return jnp.dot(a, b, preferred_element_type=F32)


def dot_nt(a, b):
    return lax.dot_general(a, b, NT, preferred_element_type=F32)


def kernel(
    nr, nc,
    q_hbm, d_hbm, k_hbm, v_hbm, pk_hbm, pv_hbm, len_ref, plen_ref,
    ov, dqv, kg_ref, vg_ref, pkg_ref, pvg_ref,
    qv, dv, k_ref, v_ref, pk_ref, pv_ref, kv, term, rterm, hidden_cols, causal_cols,
    pown, prep, pterm, psum, xsend, xrecv, pback,
    in_sem, x_sem,
    a_send, a_recv, b_send, b_recv, g_send, g_recv,
    t_send, t_recv, p_send, p_recv, z_send, z_recv,
):
    prow = 2 * nc
    prompt = nr * prow
    key_rows = prompt + nc * TOK
    r = lax.axis_index("resp")
    c = lax.axis_index("ctx")
    nm = nr // 2
    half = lax.rem(r // 2, 2)
    m = (r // 4) * 2 + lax.rem(r, 2)
    partner = r + 2 - 4 * half

    def resp_of(pair):
        return (pair // 2) * 4 + 2 * half + lax.rem(pair, 2)

    load_q = pltpu.make_async_copy(q_hbm, qv, in_sem.at[0])
    load_d = pltpu.make_async_copy(d_hbm, dv, in_sem.at[1])
    loads = [
        pltpu.make_async_copy(src, dst, in_sem.at[2 + n])
        for n, (src, dst) in enumerate(((pk_hbm, pk_ref), (pv_hbm, pv_ref), (k_hbm, k_ref), (v_hbm, v_ref)))
    ]
    for load in loads:
        load.start()
    load_q.start()
    load_d.start()

    barrier = pltpu.get_barrier_semaphore()

    def others(n, me, body):
        def step(i, carry):
            body(lax.rem(me + i, n))
            return carry

        lax.fori_loop(1, n, step, 0)

    others(nc, c, lambda p: pl.semaphore_signal(barrier, inc=1, device_id={"ctx": p}, device_id_type=MESH))
    others(nm, m, lambda p: pl.semaphore_signal(
        barrier, inc=1, device_id={"resp": resp_of(p)}, device_id_type=MESH))
    pl.semaphore_signal(barrier, inc=1, device_id={"resp": partner}, device_id_type=MESH)

    def block_rows(j):
        return pl.ds(pl.multiple_of(prompt + j * TOK, TOK), TOK)

    for load in loads:
        load.wait()
    for w, ref in enumerate((pk_ref, pv_ref)):
        wide = ref[...].astype(F32)
        rows = [wide[:, g * HD:(g + 1) * HD] for g in range(KVH)]
        pown[half, c, w] = jnp.concatenate(rows, 0).astype(BF)
    for g in range(KVH):
        kv[g, 0, block_rows(c), :] = k_ref[:, g * HD:(g + 1) * HD]
        kv[g, 1, block_rows(c), :] = v_ref[:, g * HD:(g + 1) * HD]

    pl.semaphore_wait(barrier, nc - 1 + nm)

    def copy_a(slot, peer):
        return pltpu.make_async_remote_copy(
            src_ref=pown.at[half, slot], dst_ref=pown.at[half, slot],
            send_sem=a_send.at[peer], recv_sem=a_recv.at[slot],
            device_id={"ctx": peer}, device_id_type=MESH)

    others(nc, c, lambda p: copy_a(c, p).start())

    def copy_g(n, slot, peer):
        part = kv.at[n, :, block_rows(slot), :]
        return pltpu.make_async_remote_copy(
            src_ref=part, dst_ref=part,
            send_sem=g_send.at[n, peer], recv_sem=g_recv.at[n, slot],
            device_id={"ctx": peer}, device_id_type=MESH)

    def loop(lo, hi, body):
        def step(i, carry):
            body(i)
            return carry

        lax.fori_loop(lo, hi, step, 0)

    def gather(n):
        loop(0, nc - 1 - c, lambda i: copy_g(n, c, nc - 1 - i).start())


    def clear(j):
        def one(g):
            kv[g, 0, block_rows(j), :] = jnp.zeros((TOK, HD), BF)
            kv[g, 1, block_rows(j), :] = jnp.zeros((TOK, HD), BF)
        loop(0, KVH, one)

    loop(c + 1, nc, clear)

    row = iota((key_rows, HD), 0)
    col = iota((key_rows, HD), 1)
    slot, within = row // prow, lax.rem(row, prow)
    place = ((slot // 4) * 4 + lax.rem(slot, 2) * 2 + lax.rem(slot // 2, 2)) * prow + within
    gone = ((row < prompt) & (place >= plen_ref[0])) | (row >= prompt + (c + 1) * TOK)
    diagonal = (row - (prompt + c * TOK) == col) & (col > 0)
    hidden_cols[...] = jnp.where(diagonal, 1.0, jnp.where(gone & (col == 0), HIDE, 0.0)).astype(BF)
    tok = iota((TOK, HD), 0)
    key = iota((TOK, HD), 1)
    causal_cols[...] = jnp.where(key == 0, 1.0, jnp.where(key > tok, HIDE, 0.0)).astype(BF)
    live = c * TOK + tok < len_ref[0]
    live_lane = jnp.where(c * TOK + iota((1, TOK), 1) < len_ref[0], 1.0, 0.0)

    n16 = 16 * nc

    def order(to_heads):
        a = iota((n16, n16), 0)
        b = iota((n16, n16), 1)
        if not to_heads:
            a, b = b, a
        head, rest = a // prow, lax.rem(a, prow)
        return jnp.where((rest // 2) * 16 + head * 2 + lax.rem(rest, 2) == b, 1.0, 0.0).astype(BF)

    def copy_x(which, src, dst):
        return pltpu.make_async_remote_copy(
            src_ref=src, dst_ref=dst, send_sem=x_sem.at[which, 0], recv_sem=x_sem.at[which, 1],
            device_id={"resp": partner}, device_id_type=MESH)

    to_heads = order(True)
    others(nc, c, lambda p: copy_a(p, p).wait_recv())
    gather(0)
    swap = copy_x(0, pown.at[half], pown.at[half])
    swap.start()
    swap.wait_recv()
    gather(1)

    def pair_rows(pair, h=0, count=2):
        return pl.ds(pl.multiple_of((2 * pair + h) * prow, prow), count * prow)

    for h in range(2):
        for w in range(2):
            got = jnp.concatenate([pown[h, j, w] for j in range(nc)], 0)
            mine = dot(to_heads, got).astype(BF)
            for g in range(KVH):
                kv[g, w, pair_rows(m, h, 1), :] = mine[g * prow:(g + 1) * prow]

    def copy_b(n, slot, peer):
        g0, count = PROMPT_IN[n]
        part = kv.at[pl.ds(g0, count), :, pair_rows(slot), :]
        return pltpu.make_async_remote_copy(
            src_ref=part, dst_ref=part,
            send_sem=b_send.at[n, peer], recv_sem=b_recv.at[n, slot],
            device_id={"resp": resp_of(peer)}, device_id_type=MESH)

    def prompt_in(n):
        others(nm, m, lambda p: copy_b(n, m, p).start())

    prompt_in(0)

    load_q.wait()
    load_d.wait()

    def copy_t(g, block, src):
        return pltpu.make_async_remote_copy(
            src_ref=term.at[g, :, block_rows(block), :], dst_ref=rterm.at[src, g],
            send_sem=t_send.at[g, block], recv_sem=t_recv.at[g, src],
            device_id={"ctx": block}, device_id_type=MESH)

    def copy_p(n, owner, src):
        g0, count = PROMPT_OUT[n]
        return pltpu.make_async_remote_copy(
            src_ref=term.at[pl.ds(g0, count), :, pair_rows(owner), :],
            dst_ref=pterm.at[src, pl.ds(g0, count)],
            send_sem=p_send.at[n, owner], recv_sem=p_recv.at[n, src],
            device_id={"resp": resp_of(owner)}, device_id_type=MESH)

    def sum_prompt(n):
        g0, count = PROMPT_OUT[n]
        heads = pl.ds(g0, count)
        others(nm, m, lambda p: copy_p(n, m, p).wait_recv())
        for h in range(2):
            psum[h, heads] = term[heads, :, pair_rows(m, h, 1), :].astype(F32)

        def add(p):
            for h in range(2):
                psum[h, heads] += pterm[p, heads, :, h * prow:(h + 1) * prow, :].astype(F32)

        others(nm, m, add)

    def head(g):
        for n, (g0, _) in enumerate(PROMPT_IN):
            @pl.when(g == g0)
            def _():
                others(nm, m, lambda p: copy_b(n, p, p).wait_recv())
        for n in (1, 2):
            @pl.when(g == n - 1)
            def _():
                prompt_in(n)

        @pl.when(g + 2 < KVH)
        def _():
            gather(g + 2)

        loop(0, c, lambda j: copy_g(g, j, j).wait_recv())

        cols = [pl.ds(pl.multiple_of(g * ROWS + a * HD, HD), HD) for a in range(G)]
        k = kv[g, 0]
        v = kv[g, 1]
        q = jnp.concatenate([qv[:, x] for x in cols], 0)
        d = jnp.concatenate([jnp.where(live, dv[:, x], jnp.zeros((), BF)) for x in cols], 0)
        limit = jnp.concatenate([causal_cols[...]] * G, 0)
        s = dot_nt(jnp.concatenate([k, hidden_cols[...]], 1), jnp.concatenate([q, limit], 1))
        dp = dot_nt(v, d)
        top = jnp.max(s, 0, keepdims=True)
        p = jnp.exp2((s - top) * (SCALE * LOG2E))
        inv = 1.0 / jnp.sum(p, 0, keepdims=True)
        p = p.astype(BF)
        out = (dot(v.T, p) * (inv * jnp.concatenate([live_lane] * G, 1))).astype(BF)
        corr = jnp.sum(d.T.astype(F32) * out.astype(F32), 0, keepdims=True)
        out = out.T
        for a in range(G):
            ov[:, cols[a]] = out[a * TOK:(a + 1) * TOK]
        ds = p * (dp - corr).astype(BF)
        inv_col = jnp.broadcast_to(inv, (HD, ROWS)).T
        term[g, 1] = dot(p, (d.astype(F32) * inv_col).astype(BF)).astype(BF)
        term[g, 0] = dot(ds, (q.astype(F32) * (inv_col * SCALE)).astype(BF)).astype(BF)
        loop(0, c, lambda j: copy_t(g, j, c).start())
        dq = (dot(k.T, ds) * (inv * SCALE)).T.astype(BF)
        for a in range(G):
            dqv[:, cols[a]] = dq[a * TOK:(a + 1) * TOK]
        for n, (g0, count) in enumerate(PROMPT_OUT):
            @pl.when(g == g0 + count - 1)
            def _():
                others(nm, m, lambda p: copy_p(n, p, m).start())

        @pl.when(g == 6)
        def _():
            sum_prompt(0)

    loop(0, KVH, head)

    sum_prompt(1)
    sum_prompt(2)
    xsend[...] = psum[1 - half].astype(BF)
    swap_back = copy_x(1, xsend, xrecv)
    swap_back.start()
    swap_back.wait_recv()
    psum[half] += xrecv[...].astype(F32)
    from_heads = order(False)
    for w in range(2):
        part = jnp.concatenate([psum[half, g, w] for g in range(KVH)], 0).astype(BF)
        part = dot(from_heads, part).astype(BF)
        for j in range(nc):
            prep[j, w] = part[16 * j:16 * (j + 1)]

    def copy_z(owner, src):
        return pltpu.make_async_remote_copy(
            src_ref=prep.at[owner], dst_ref=pback.at[src],
            send_sem=z_send.at[owner], recv_sem=z_recv.at[src],
            device_id={"ctx": owner}, device_id_type=MESH)

    others(nc, c, lambda p: copy_z(p, c).start())

    for g in range(KVH):
        loop(c + 1, nc, lambda src: copy_t(g, c, src).wait_recv())
        for w, ref in enumerate((kg_ref, vg_ref)):
            ref[:, g * HD:(g + 1) * HD] = lax.fori_loop(
                c + 1, nc, lambda src, total: total + rterm[src, g, w].astype(F32),
                term[g, w, block_rows(c), :].astype(F32))

    others(nc, c, lambda p: copy_z(c, p).wait_recv())
    for w, ref in enumerate((pkg_ref, pvg_ref)):
        total = prep[c, w].astype(F32)
        for i in range(1, nc):
            total += pback[lax.rem(c + i, nc), w].astype(F32)
        for g in range(KVH):
            ref[:, g * HD:(g + 1) * HD] = total[2 * g:2 * g + 2]

    others(nc, c, lambda p: copy_a(c, p).wait_send())
    swap.wait_send()
    swap_back.wait_send()
    for n in range(len(PROMPT_IN)):
        others(nm, m, lambda p: copy_b(n, m, p).wait_send())
    for n in range(len(PROMPT_OUT)):
        others(nm, m, lambda p: copy_p(n, p, m).wait_send())
    others(nc, c, lambda p: copy_z(p, c).wait_send())
    def finish(g):
        loop(c + 1, nc, lambda p: copy_g(g, c, p).wait_send())
        loop(0, c, lambda j: copy_t(g, j, c).wait_send())

    loop(0, KVH, finish)


def per_device(
    nr, nc, queries, resp_keys, resp_values, prompt_keys, prompt_values, upstream, lengths, prompt_length
):
    prow = 2 * nc
    key_rows = nr * prow + nc * TOK
    width = KVH * HD
    vmem = pl.BlockSpec(memory_space=pltpu.VMEM)
    smem = pl.BlockSpec(memory_space=pltpu.SMEM)
    hbm = pl.BlockSpec(memory_space=pltpu.HBM)
    dma = pltpu.SemaphoreType.DMA
    big = jax.ShapeDtypeStruct((TOK, KVH * ROWS), BF)
    grad = jax.ShapeDtypeStruct((TOK, width), F32)
    small = jax.ShapeDtypeStruct((2, width), F32)
    outs = pl.pallas_call(
        functools.partial(kernel, nr, nc),
        out_shape=(big, big, grad, grad, small, small),
        in_specs=[hbm] * 6 + [smem, smem],
        out_specs=[vmem] * 6,
        scratch_shapes=[
            pltpu.VMEM((TOK, KVH * ROWS), BF),
            pltpu.VMEM((TOK, KVH * ROWS), BF),
            pltpu.VMEM((TOK, width), BF),
            pltpu.VMEM((TOK, width), BF),
            pltpu.VMEM((2, width), BF),
            pltpu.VMEM((2, width), BF),
            pltpu.VMEM((KVH, 2, key_rows, HD), BF),
            pltpu.VMEM((KVH, 2, key_rows, HD), BF),
            pltpu.VMEM((nc, KVH, 2, TOK, HD), BF),
            pltpu.VMEM((key_rows, HD), BF),
            pltpu.VMEM((TOK, HD), BF),
            pltpu.VMEM((2, nc, 2, 16, HD), BF),
            pltpu.VMEM((nc, 2, 16, HD), BF),
            pltpu.VMEM((nr // 2, KVH, 2, 2 * prow, HD), BF),
            pltpu.VMEM((2, KVH, 2, prow, HD), F32),
            pltpu.VMEM((KVH, 2, prow, HD), BF),
            pltpu.VMEM((KVH, 2, prow, HD), BF),
            pltpu.VMEM((nc, 2, 16, HD), BF),
            dma((6,)), dma((2, 2)),
            dma((nc,)), dma((nc,)),
            dma((len(PROMPT_IN), nr // 2)), dma((len(PROMPT_IN), nr // 2)),
            dma((KVH, nc)), dma((KVH, nc)),
            dma((KVH, nc)), dma((KVH, nc)),
            dma((len(PROMPT_OUT), nr // 2)), dma((len(PROMPT_OUT), nr // 2)),
            dma((nc,)), dma((nc,)),
        ],
        compiler_params=pltpu.CompilerParams(
            collective_id=0, has_side_effects=True, vmem_limit_bytes=58 * 2**20),
        cost_estimate=pl.CostEstimate(
            flops=12 * KVH * ROWS * key_rows * HD, bytes_accessed=10 * 2**20,
            transcendentals=KVH * ROWS * key_rows),
    )(
        queries[0], upstream[0], resp_keys[0], resp_values[0],
        prompt_keys, prompt_values, lengths, prompt_length,
    )
    attended, query_grads, key_grads, value_grads, pkg, pvg = outs
    return (
        attended[None], query_grads[None], key_grads[None], value_grads[None],
        pkg, pvg,
    )


def solution(mesh):
    tokens = P("resp", "ctx", None)
    rows = P(("resp", "ctx"), None)
    return jax.shard_map(
        functools.partial(per_device, mesh.shape["resp"], mesh.shape["ctx"]),
        mesh=mesh,
        in_specs=(tokens, tokens, tokens, rows, rows, tokens, P("resp"), P()),
        out_specs=(tokens, tokens, tokens, tokens, rows, rows),
        check_vma=False,
    )
```
